128 devices in a mesh: head: 8 (over x, core), ctx: 16 (over z, y).
Axes of the slice: x: 4, y: 4, z: 4, core: 2. Of those that a mesh axis runs over, the one named last changes fastest.
Arguments:
- queries: bfloat16 [128, 256, 4096], P('ctx', 'head'), may hold values from -6 to 6
- keys: bfloat16 [128, 256, 4096], P('ctx', 'head'), may hold values from -6 to 6
- values: bfloat16 [128, 256, 4096], P('ctx', 'head'), may hold values from -6 to 6
- grad_out: bfloat16 [128, 256, 4096], P('ctx', 'head'), may hold values from -24 to 24
- attn_out: bfloat16 [128, 256, 4096], P('ctx', 'head'), may hold values from -6 to 6
- lse: float32 [128, 32, 256], P('ctx', 'head'), may hold values from 5.5 to 7.5
- selected: int32 [128, 2], P('ctx'), may hold values from 0 to 119, as said below
- doc_lengths: int32 [4], replicated, may hold values from 1 to 32640, 32768 in all
Outputs:
- grad_q: bfloat16 [128, 256, 4096], P('ctx', None, 'head')
- grad_k: bfloat16 [128, 256, 4096], P('ctx', None, 'head')
- grad_v: bfloat16 [128, 256, 4096], P('ctx', None, 'head')
The draws below stay inside these ranges and needn't reach their ends.
Inputs may be any that keep to these rules, and one draw needn't show every extreme that they name: `selected`: for query block i either both entries equal i (it selects nothing) or they are two different blocks j with the same o = j // 8, and o < i // 8. Among the 8 query blocks with one value of i // 8, at most 1 select blocks of any one o, and 1 is reached. For every value of i // 8 from 1 on, some query block selects blocks with o = 0.
All inputs are finite; a program needn't handle non-finite values.
Results may differ from the reference program's by a relative error of at most 0.0055.
Values may be sent and summed in bfloat16 or wider, within the bound.
A program may use at most 192 MiB of HBM per device.

```python
import math
import jax
import jax.numpy as jnp
import numpy as np
from jax import lax

H = 32
HD = 128
BLK = 256
QB_DEV = 8
DOCS = 4
NB = 128
TOKENS = 32768


def draw_selected(key, part):
    key = jax.random.fold_in(key, 7)
    ctx_count = NB // QB_DEV
    spread = min(QB_DEV, ctx_count - 1)

    def one_device(device):
        subkey = jax.random.fold_in(key, device)
        key_perm, key_spot, key_order, key_first, key_second = jax.random.split(subkey, 5)
        perm = jax.random.permutation(key_perm, ctx_count - 1).astype(jnp.int32)
        spot = jax.random.randint(key_spot, (), 0, spread, dtype=jnp.int32)
        zero_at = jnp.argmax(perm == 0).astype(jnp.int32)
        moved = perm[spot]
        perm = perm.at[zero_at].set(moved).at[spot].set(0)
        top_pos = (spot + 1) % spread
        top_at = jnp.argmax(perm == ctx_count - 2).astype(jnp.int32)
        displaced = perm[top_pos]
        perm = perm.at[top_at].set(displaced).at[top_pos].set(ctx_count - 2)
        order = jax.random.permutation(key_order, QB_DEV).astype(jnp.int32)
        owner = perm[order % (ctx_count - 1)]
        first = jax.random.randint(key_first, (QB_DEV,), 0, QB_DEV, dtype=jnp.int32)
        first = jnp.where(order == top_pos, QB_DEV - 1, first)
        second = (first + 1 + jax.random.randint(key_second, (QB_DEV,), 0, QB_DEV - 1, dtype=jnp.int32)) % QB_DEV
        own_ids = device * QB_DEV + jnp.arange(QB_DEV, dtype=jnp.int32)
        used = owner < device
        entry_one = jnp.where(used, owner * QB_DEV + first, own_ids)
        entry_two = jnp.where(used, owner * QB_DEV + second, own_ids)
        return jnp.stack([entry_one, entry_two], axis=1)
    return jax.vmap(one_device)(jnp.arange(ctx_count, dtype=jnp.int32)).reshape(NB, 2)


def block_scale(key, dims, shards, smallest, largest):
    gain = 1.0
    for dim, shards_of in shards:
        heights = jax.random.uniform(jax.random.fold_in(jax.random.fold_in(key, 6), dim), (shards_of,), jnp.float32, smallest / len(shards), largest / len(shards))
        gain = gain * jnp.repeat(jnp.exp(heights), dims[dim] // shards_of).reshape((-1,) + (1,) * (len(dims) - 1 - dim))
    return gain


def profile(amount, total, reach, skew):
    loads = [(1 << 20) // math.isqrt(standing ** skew) + 1 for standing in range(2, amount + 1)]
    surplus, counts = total - reach - (amount - 1), [1] * (amount - 1)
    while surplus > 0:
        candidates = [i for i in range(amount - 1) if counts[i] < reach]
        mass, remaining = sum([loads[i] for i in candidates]), surplus
        for i in candidates:
            addition = min(reach - counts[i], max(1, remaining * loads[i] // mass), surplus)
            counts[i] = counts[i] + addition
            surplus = surplus - addition
    return np.array([reach] + counts)


def uneven(stream_key, number_of, total, most, slope):
    if number_of == 2:
        one = jax.random.randint(stream_key, (), max(1, total - most), min(most, total - 1) + 1)
        return jnp.stack([one, total - one])
    sizes = jnp.asarray(profile(number_of, total, most, slope), jnp.int32)
    twos = (number_of - 1) // 2
    source_of, receiver = sizes[1:1 + 2 * twos:2], sizes[2:2 + 2 * twos:2]
    slack = jnp.minimum(source_of - 1, most - receiver)
    passed = jax.random.randint(jax.random.fold_in(stream_key, 1), (twos,), 0, 1 << 20) % (slack + 1)
    sizes = sizes.at[1:1 + 2 * twos:2].set(source_of - passed).at[2:2 + 2 * twos:2].set(receiver + passed)
    return sizes[jax.random.permutation(jax.random.fold_in(stream_key, 2), number_of)]


def scatter_about(rng, dims, deviation, reach, pieces=(), held_as=jnp.bfloat16):
    values = deviation * jax.random.normal(rng, dims, jnp.float32)
    if pieces:
        values = values * block_scale(rng, dims, pieces, -0.22, 0.18)
    return jnp.clip(values, -reach, reach).astype(held_as)


def setup_inputs(seed: int = 0) -> dict:
    streams_of = jax.random.split(jax.random.key(seed), 9)
    return {
        "queries": scatter_about(streams_of[0], (NB, BLK, H * HD), 1.0, 6.0, ((0, 16), (1, 8))),
        "keys": scatter_about(streams_of[1], (NB, BLK, H * HD), 1.0, 6.0, ((0, 16), (1, 8))),
        "values": scatter_about(streams_of[2], (NB, BLK, H * HD), 1.0, 6.0, ((0, 16), (1, 8))),
        "grad_out": scatter_about(streams_of[3], (NB, BLK, H * HD), 4.0, 24.0, ((0, 16), (1, 8))),
        "attn_out": scatter_about(streams_of[4], (NB, BLK, H * HD), 1.0, 6.0, ((0, 16), (1, 8))),
        "lse": jnp.clip(5.5 + 2.0 * jax.random.uniform(streams_of[5], (NB, H, BLK), jnp.float32) ** block_scale(streams_of[5], (NB, H, BLK), ((0, 16), (1, 8)), -0.2, 0.2), 5.5, 7.5),
        "selected": draw_selected(jax.random.fold_in(streams_of[8], 71), 0),
        "doc_lengths": uneven(streams_of[7], DOCS, TOKENS, TOKENS - BLK // 2, 2).astype(jnp.int32),
    }


def doc_of(positions, doc_lengths):
    ends = jnp.cumsum(doc_lengths).astype(jnp.int32)
    return jnp.sum((positions[..., None] >= ends).astype(jnp.int32), axis=-1)


def reference(queries, keys, values, grad_out, attn_out, lse, selected, doc_lengths):
    scale = HD ** -0.5
    rows = jnp.arange(BLK, dtype=jnp.int32)
    key_index = jnp.arange(3 * BLK, dtype=jnp.int32)

    def one_block(carry, block):
        acc_keys, acc_values = carry
        picks = selected[block].astype(jnp.int32)
        ids = jnp.concatenate([block[None].astype(jnp.int32), picks])
        used = jnp.concatenate([jnp.ones((1,), dtype=bool), picks != block])
        query = queries[block].reshape(BLK, H, HD).astype(jnp.float32)
        grad = grad_out[block].reshape(BLK, H, HD).astype(jnp.float32)
        output = attn_out[block].reshape(BLK, H, HD).astype(jnp.float32)
        key_rows = keys[ids].reshape(3 * BLK, H, HD).astype(jnp.float32)
        value_rows = values[ids].reshape(3 * BLK, H, HD).astype(jnp.float32)
        query_docs = doc_of(block * BLK + rows, doc_lengths)
        key_docs = doc_of((ids[:, None] * BLK + rows[None, :]).reshape(-1), doc_lengths)
        used_keys = jnp.repeat(used, BLK)
        allowed = (query_docs[:, None] == key_docs[None, :]) & used_keys[None, :]
        allowed = allowed & ((key_index[None, :] >= BLK) | (rows[:, None] >= key_index[None, :]))
        scores = jnp.einsum('rhd,khd->hrk', query, key_rows) * scale
        probs = jnp.where(allowed[None], jnp.exp(scores - lse[block][:, :, None]), 0.0)
        prob_low = lax.optimization_barrier(probs.astype(jnp.bfloat16)).astype(jnp.float32)
        delta = jnp.transpose(jnp.sum(grad * output, axis=-1))
        dprobs = jnp.einsum('rhd,khd->hrk', grad, value_rows)
        dscores = lax.optimization_barrier((probs * (dprobs - delta[:, :, None])).astype(jnp.bfloat16)).astype(jnp.float32)
        grad_query = (jnp.einsum('hrk,khd->rhd', dscores, key_rows) * scale).reshape(BLK, H * HD).astype(jnp.bfloat16)
        part_keys = (jnp.einsum('hrk,rhd->khd', dscores, query) * scale).reshape(3, BLK, H * HD)
        part_values = jnp.einsum('hrk,rhd->khd', prob_low, grad).reshape(3, BLK, H * HD)
        far_keys = lax.optimization_barrier(part_keys[1:].astype(jnp.bfloat16)).astype(jnp.float32)
        far_values = lax.optimization_barrier(part_values[1:].astype(jnp.bfloat16)).astype(jnp.float32)
        acc_keys = acc_keys.at[picks].add(far_keys)
        acc_values = acc_values.at[picks].add(far_values)
        return (acc_keys, acc_values), (grad_query, part_keys[0], part_values[0])

    zeros = jnp.zeros((NB, BLK, H * HD), jnp.float32)
    (acc_keys, acc_values), (grad_q, own_keys, own_values) = lax.scan(one_block, (zeros, zeros), jnp.arange(NB, dtype=jnp.int32))
    grad_k = (own_keys + acc_keys).astype(jnp.bfloat16)
    grad_v = (own_values + acc_values).astype(jnp.bfloat16)
    return (grad_q, grad_k, grad_v)
```

```python
import functools
import math

import jax
import jax.numpy as jnp
from jax import lax
from jax.experimental import pallas as pl
from jax.experimental.pallas import tpu as pltpu
from jax.sharding import PartitionSpec as P

MESH = pl.DeviceIdType.MESH
F32, BF16, I32 = jnp.float32, jnp.bfloat16, jnp.int32


def dot(left, right, left_dim, right_dim):
    return lax.dot_general(
        left, right, (((left_dim,), (right_dim,)), ((), ())), preferred_element_type=F32
    )


def loop(low, high, func):
    def step(index, carry):
        func(index)
        return carry

    lax.fori_loop(low, high, step, 0)


def iota(shape, dim):
    return lax.broadcasted_iota(I32, shape, dim)


def grads(query, grad, key, value, lse_row, delta_row, allowed, scale):
    scores = dot(key, query, 1, 1) * scale
    probs = jnp.where(allowed, jnp.exp(scores - lse_row), 0.0)
    dprobs = dot(value, grad, 1, 1)
    dscores = (probs * (dprobs - delta_row)).astype(BF16)
    part_value = dot(probs.astype(BF16), grad, 1, 0)
    part_key = dot(dscores, query, 1, 0) * scale
    grad_query = dot(dscores, key, 0, 0) * scale
    return grad_query, part_key, part_value


def kernel(
    nh, nc, B, R, D, S, lane_rows,
    q_ref, k_ref, v_ref, g_ref, o_ref, lse_ref, selpad_ref, sel_ref, docs_ref,
    gq_out, gk_out, gv_out,
    xq, xk, xv, xg, curq, curk, curv, curg, snd, far, gqs, gqr, curr, gqown, parts, own, run,
    stage, go, dsend, dr, dl, auxs, auxr, selall, meta, meta_s, bsel,
    xs, xr, xl, fs, fr, gs, gr, ds, dsr, as_, ar, ss, sr, os_, ls,
):
    h, c = lax.axis_index("head"), lax.axis_index("ctx")
    rows = R // nh
    scale = D ** (-0.5)
    shift = int(math.log2(B))
    lanes = 128

    selall[...] = jnp.full(selall.shape, -1, I32)
    curr[pl.ds(c, 1)] = jnp.zeros((1, R, D), BF16)

    barrier = pltpu.get_barrier_semaphore()

    def greet_head(n):
        pl.semaphore_signal(barrier, inc=1, device_id=(lax.rem(h + n, nh), c), device_id_type=MESH)

    def greet_ctx(n):
        pl.semaphore_signal(barrier, inc=1, device_id=(h, lax.rem(c + n, nc)), device_id_type=MESH)

    loop(1, nh, greet_head)
    loop(1, nc, greet_ctx)
    pl.semaphore_wait(barrier, nh + nc - 2)

    sources, places = (q_ref, g_ref, k_ref, v_ref), (xq, xg, xk, xv)

    def columns(to, s):
        return pl.ds(pl.multiple_of(to * (S * D) + s * D, D), D)

    here = pl.ds(pl.multiple_of(h * rows, rows), rows)

    def head_copy(a, s, n):
        to = lax.rem(h + n, nh)
        return pltpu.make_async_remote_copy(
            src_ref=sources[a].at[:, :, columns(to, s)],
            dst_ref=places[a].at[s, :, here, :],
            send_sem=xs.at[a, s, n],
            recv_sem=xr.at[a, s, n],
            device_id=(to, c),
            device_id_type=MESH,
        )

    def head_local(a, s):
        return pltpu.make_async_copy(
            sources[a].at[:, :, columns(h, s)], places[a].at[s, :, here, :], xl.at[a, s]
        )

    def head_start(pair, s):
        for a in pair:
            loop(1, nh, lambda n: head_copy(a, s, n).start())
            head_local(a, s).start()

    def head_wait(pair, s):
        for a in pair:
            loop(1, nh, lambda n: head_copy(a, s, n).wait_recv())
            head_local(a, s).wait()

    go_copies = [
        pltpu.make_async_copy(ref, go.at[n], ls.at[n]) for n, ref in enumerate((g_ref, o_ref))
    ]
    for copy in go_copies:
        copy.start()

    def sel_copy(n, to):
        return pltpu.make_async_remote_copy(
            src_ref=selpad_ref, dst_ref=selall.at[c], send_sem=ss.at[n], recv_sem=sr.at[n],
            device_id=(h, to), device_id_type=MESH,
        )

    def up(n):
        return lax.rem(c + n, nc)

    def down(n):
        return lax.rem(c + nc - n, nc)

    loop(1, c + 1, lambda n: sel_copy(n, down(n)).start())

    head_start((0, 1), 0)
    head_start((0, 1), 1)

    def find(owner):
        found = 0
        for b in range(B):
            found = found + jnp.where(sel_ref[b, 0] // B == owner, b, 0)
        bsel[owner] = jnp.minimum(found, B - 1)

    loop(0, c, find)

    for copy in go_copies:
        copy.wait()
    pick = (iota((8, S * D), 1) // D == iota((8, S * D), 0)).astype(BF16)

    def delta_rows(to):
        cols = pl.ds(pl.multiple_of(to * (S * D), S * D), S * D)
        prod = go[0, :, :, cols].astype(F32) * go[1, :, :, cols].astype(F32)
        prod = prod.reshape(B * rows, S * D)
        high = prod.astype(BF16)
        low = (prod - high.astype(F32)).astype(BF16)
        dsend[to] = dot(pick, high, 1, 1) + dot(pick, low, 1, 1)

    loop(0, nh, delta_rows)

    def delta_copy(n):
        to = lax.rem(h + n, nh)
        return pltpu.make_async_remote_copy(
            src_ref=dsend.at[to], dst_ref=dr.at[h], send_sem=ds.at[n], recv_sem=dsr.at[n],
            device_id=(to, c), device_id_type=MESH,
        )

    loop(1, nh, lambda n: delta_copy(n).start())
    dr[pl.ds(h, 1)] = dsend[pl.ds(h, 1)]
    loop(1, nh, lambda n: delta_copy(n).wait_recv())
    for b in range(B):
        dl[b] = jnp.concatenate(
            [dr[n][:, b * rows : (b + 1) * rows] for n in range(nh)], axis=1
        )

    def aux_copy(n, to):
        return pltpu.make_async_remote_copy(
            src_ref=auxs.at[to], dst_ref=auxr.at[c], send_sem=as_.at[n], recv_sem=ar.at[n],
            device_id=(h, to), device_id_type=MESH,
        )

    def aux_send(n):
        to = down(n)
        b = bsel[to]
        auxs[to, 0:S, :] = lse_ref[b]
        auxs[to, S : 2 * S, :] = dl[b][0:S]
        aux_copy(n, to).start()

    loop(1, c + 1, aux_send)

    def far_copy(s, n, to):
        return pltpu.make_async_remote_copy(
            src_ref=snd.at[lax.rem(s, 2), to], dst_ref=far.at[s, c],
            send_sem=fs.at[s, n], recv_sem=fr.at[s, n], device_id=(h, to), device_id_type=MESH,
        )

    def gather(s):
        head_wait((0, 1), s)

        @pl.when(s < S - 2)
        def _():
            head_start((0, 1), s + 2)

        @pl.when(s == S - 2)
        def _():
            head_start((2, 3), 0)

        @pl.when(s == S - 1)
        def _():
            loop(1, S, lambda t: head_start((2, 3), t))

        @pl.when(s >= 2)
        def _():
            loop(1, c + 1, lambda n: far_copy(s - 2, n, down(n)).wait_send())

        curq[...] = xq[s]
        curg[...] = xg[s]

        def one(n):
            to = down(n)
            b = bsel[to]
            snd[lax.rem(s, 2), to, 0] = curq[b]
            snd[lax.rem(s, 2), to, 1] = curg[b]
            far_copy(s, n, to).start()

        loop(1, c + 1, one)

    loop(0, S, gather)

    loop(1, nc - c, lambda n: sel_copy(n, up(n)).wait_recv())
    picks = selall[...]
    hit = (picks >> shift) == c
    block_sum = lambda terms: jnp.sum(jnp.where(hit, terms, 0), axis=1)
    used = block_sum(jnp.ones_like(picks))
    local = block_sum(picks & (B - 1))
    which = block_sum(iota(picks.shape, 1))
    source, lane = iota((nc, lanes), 0), iota((nc, lanes), 1)
    order = jnp.where(used > 0, local, B)
    order = jnp.where(source > c, order, B + 1)

    def across(column):
        return jnp.sum(jnp.where(lane == source, column, 0), axis=0, keepdims=True)

    def total(terms):
        return jnp.sum(terms.astype(I32), axis=1, keepdims=True)

    inside = lane < nc
    full = [order[:, e : e + 1] * (4 * nc) + 2 * source[:, :1] + e for e in range(2)]
    full_rows = [across(column) for column in full]
    ranks = [
        sum(total((row < column) & inside) for row in full_rows) for column in full
    ]
    rank_rows = [across(column) for column in ranks]
    order_rows = [across(order[:, e : e + 1]) for e in range(2)]
    spot, spot_lane = iota((2 * nc, lanes), 0), iota((2 * nc, lanes), 1)
    at = [(row == spot) & (spot_lane < nc) for row in rank_rows]
    unit_at = sum(total(jnp.where(at[e], 2 * spot_lane + e, 0)) for e in range(2))
    block_at = sum(total(jnp.where(at[e], order_rows[e], 0)) for e in range(2))
    block, block_lane = iota((8, lanes), 0), iota((8, lanes), 1)
    last = sum(total((row <= block) & (block_lane < nc)) for row in order_rows) - 1
    has = sum(total((row == block) & (block_lane < nc)) for row in order_rows)

    def table(shape_lane, items):
        out = jnp.zeros(shape_lane.shape, I32)
        for n, item in enumerate(items):
            out = jnp.where(shape_lane == n, item, out)
        return out

    meta[0 : 2 * nc] = table(spot_lane, (unit_at, block_at))
    meta[2 * nc : 3 * nc] = table(
        lane, (local[:, 0:1], local[:, 1:2], used[:, 0:1], which[:, 0:1])
    )
    meta[3 * nc : 3 * nc + 8] = table(block_lane, (jnp.maximum(last, 0), has))
    to_scalar = pltpu.make_async_copy(meta, meta_s, ls.at[0])
    to_scalar.start()
    to_scalar.wait()

    loop(1, nc - c, lambda n: aux_copy(n, up(n)).wait_recv())

    def doc_of(positions):
        end, doc = 0, jnp.zeros(positions.shape, I32)
        for n in range(docs_ref.shape[0]):
            end = end + docs_ref[n]
            doc = doc + (positions >= end).astype(I32)
        return doc

    row_lane, row_sub = iota((1, R), 1), iota((R, 1), 0)
    causal = row_sub <= row_lane

    def back_copy(s, n, to):
        return pltpu.make_async_remote_copy(
            src_ref=gqs.at[s, to], dst_ref=gqr.at[s, c], send_sem=gs.at[s, n],
            recv_sem=gr.at[s, n], device_id=(h, to), device_id_type=MESH,
        )

    def out_copy(s, n):
        ref = (gq_out, gk_out, gv_out)[n]
        return pltpu.make_async_copy(
            stage.at[s, n], ref.at[:, :, pl.ds(pl.multiple_of(s * D, D), D)], os_.at[s, n]
        )

    def finish_query(s):
        def one(n):
            back_copy(s, n, down(n)).wait_recv()
            curr[pl.ds(down(n), 1)] = gqr[s, pl.ds(down(n), 1)]

        loop(1, c + 1, one)

        def add(b):
            owner = (sel_ref[b, 0] // B) & (nc - 1)
            stage[s, 0, b] = (gqown[s, b] + curr[owner].astype(F32)).astype(BF16)

        loop(0, B, add)
        out_copy(s, 0).start()

    def heads(s):
        head_wait((2, 3), s)
        curk[...] = xk[s]
        curv[...] = xv[s]

        def own_block(b):
            docs_lane = doc_of((c * B + b) * R + row_lane)
            docs_sub = doc_of((c * B + b) * R + row_sub)
            allowed = causal & (docs_lane == docs_sub)
            grad_query, part_key, part_value = grads(
                xq[s, b], xg[s, b], xk[s, b], xv[s, b],
                lse_ref[b, pl.ds(s, 1), :], dl[b, pl.ds(s, 1), :], allowed, scale,
            )
            gqown[s, b] = grad_query
            own[0, b] = part_key
            own[1, b] = part_value

        loop(0, B, own_block)

        def far_block(n):
            d = up(n)
            far_copy(s, n, up(n)).wait_recv()
            used_here = meta_s[2 * nc + d, 2] > 0
            docs_lane = doc_of((d * B + meta_s[2 * nc + d, 3]) * R + row_lane)
            keys, values, docs_sub = [], [], []
            for e in range(2):
                j = meta_s[2 * nc + d, e] & (B - 1)
                keys.append(curk[j])
                values.append(curv[j])
                docs_sub.append(
                    jnp.where(used_here, doc_of((c * B + j) * R + row_sub), -1)
                )
            allowed = jnp.concatenate(docs_sub, axis=0) == docs_lane
            grad_query, part_key, part_value = grads(
                far[s, d, 0], far[s, d, 1],
                jnp.concatenate(keys, axis=0), jnp.concatenate(values, axis=0),
                auxr[d, pl.ds(s, 1), :], auxr[d, pl.ds(S + s, 1), :], allowed, scale,
            )
            gqs[s, d] = grad_query.astype(BF16)
            back_copy(s, n, d).start()
            for e in range(2):
                parts[0, 2 * d + e] = part_key[e * R : (e + 1) * R].astype(BF16)
                parts[1, 2 * d + e] = part_value[e * R : (e + 1) * R].astype(BF16)

        loop(1, nc - c, far_block)

        for w in range(2):
            def add_hit(m, total_so_far):
                unit, j = meta_s[m, 0] & (2 * nc - 1), meta_s[m, 1]
                before = jnp.where(m == 0, -1, meta_s[jnp.maximum(m - 1, 0), 1])
                base = jnp.where(j == before, total_so_far, own[w, j & (B - 1)])
                total_now = base + parts[w, unit].astype(F32)
                run[m] = total_now.astype(BF16)
                return total_now

            lax.fori_loop(0, 2 * (nc - 1 - c), add_hit, jnp.zeros((R, D), F32))

            def settle(j):
                reached = meta_s[3 * nc + j, 1] > 0
                stage[s, 1 + w, j] = jnp.where(
                    reached, run[meta_s[3 * nc + j, 0] & (2 * nc - 1)], own[w, j].astype(BF16)
                )

            loop(0, B, settle)
            out_copy(s, 1 + w).start()

        @pl.when(s > 0)
        def _():
            finish_query(s - 1)

    loop(0, S, heads)
    finish_query(S - 1)

    loop(1, c + 1, lambda n: sel_copy(n, down(n)).wait_send())
    loop(1, c + 1, lambda n: aux_copy(n, down(n)).wait_send())
    loop(1, nh, lambda n: delta_copy(n).wait_send())

    def drain(s):
        for a in range(4):
            loop(1, nh, lambda n: head_copy(a, s, n).wait_send())
        loop(1, nc - c, lambda n: back_copy(s, n, up(n)).wait_send())
        for n in range(3):
            out_copy(s, n).wait()

        @pl.when(s >= S - 2)
        def _():
            loop(1, c + 1, lambda n: far_copy(s, n, down(n)).wait_send())

    loop(0, S, drain)


def body(queries, keys, values, grad_out, attn_out, lse, selected, doc_lengths):
    B, rows, columns = queries.shape
    S = lse.shape[1]
    nh, nc = lax.axis_size("head"), lax.axis_size("ctx")
    D = columns // (S * nh)
    R = rows * nh
    selpad = jnp.pad(selected, ((0, 0), (0, 128 - selected.shape[1])))
    any_, vmem, smem = (
        pl.BlockSpec(memory_space=space) for space in (pl.ANY, pltpu.VMEM, pltpu.SMEM)
    )
    out = jax.ShapeDtypeStruct((B, R, S * D), BF16)
    dma = pltpu.SemaphoreType.DMA
    block = (R, D)
    scratch = [
        pltpu.VMEM((S, B) + block, BF16),
        pltpu.VMEM((S, B) + block, BF16),
        pltpu.VMEM((S, B) + block, BF16),
        pltpu.VMEM((S, B) + block, BF16),
        pltpu.VMEM((B,) + block, BF16),
        pltpu.VMEM((B,) + block, BF16),
        pltpu.VMEM((B,) + block, BF16),
        pltpu.VMEM((B,) + block, BF16),
        pltpu.VMEM((2, nc, 2) + block, BF16),
        pltpu.VMEM((S, nc, 2) + block, BF16),
        pltpu.VMEM((S, nc) + block, BF16),
        pltpu.VMEM((S, nc) + block, BF16),
        pltpu.VMEM((nc,) + block, BF16),
        pltpu.VMEM((S, B) + block, F32),
        pltpu.VMEM((2, 2 * nc) + block, BF16),
        pltpu.VMEM((2, B) + block, F32),
        pltpu.VMEM((2 * nc,) + block, BF16),
        pltpu.VMEM((S, 3, B) + block, BF16),
        pltpu.VMEM((2, B, rows, columns), BF16),
        pltpu.VMEM((nh, 8, B * rows), F32),
        pltpu.VMEM((nh, 8, B * rows), F32),
        pltpu.VMEM((B, 8, R), F32),
        pltpu.VMEM((nc, 2 * S, R), F32),
        pltpu.VMEM((nc, 2 * S, R), F32),
        pltpu.VMEM((nc, B, 128), I32),
        pltpu.VMEM((3 * nc + 8, 128), I32),
        pltpu.SMEM((3 * nc + 8, 128), I32),
        pltpu.SMEM((nc,), I32),
        dma((4, S, nh)),
        dma((4, S, nh)),
        dma((4, S)),
        dma((S, nc)),
        dma((S, nc)),
        dma((S, nc)),
        dma((S, nc)),
        dma((nh,)),
        dma((nh,)),
        dma((nc,)),
        dma((nc,)),
        dma((nc,)),
        dma((nc,)),
        dma((S, 3)),
        dma((2,)),
    ]
    return pl.pallas_call(
        functools.partial(kernel, nh, nc, B, R, D, S, 128),
        out_shape=(out, out, out),
        in_specs=[any_, any_, any_, any_, any_, vmem, vmem, smem, smem],
        out_specs=(any_, any_, any_),
        scratch_shapes=scratch,
        compiler_params=pltpu.CompilerParams(
            collective_id=0, has_side_effects=True, vmem_limit_bytes=60 * 2**20
        ),
        name="block_grads",
    )(queries, keys, values, grad_out, attn_out, lse, selpad, selected, doc_lengths)


def solution(mesh):
    rows = P("ctx", "head", None)
    in_specs = (rows, rows, rows, rows, rows, rows, P("ctx", None), P())
    out_specs = (P("ctx", None, "head"),) * 3
    return jax.shard_map(body, mesh=mesh, in_specs=in_specs, out_specs=out_specs, check_vma=False)
```

```python
import functools
import math

import jax
import jax.numpy as jnp
from jax import lax
from jax.experimental import pallas as pl
from jax.experimental.pallas import tpu as pltpu
from jax.sharding import PartitionSpec as P

MESH = pl.DeviceIdType.MESH
F32, BF16, I32 = jnp.float32, jnp.bfloat16, jnp.int32


def dot(left, right, left_dim, right_dim):
    return lax.dot_general(
        left, right, (((left_dim,), (right_dim,)), ((), ())), preferred_element_type=F32
    )


def loop(low, high, func):
    def step(index, carry):
        func(index)
        return carry

    lax.fori_loop(low, high, step, 0)


def iota(shape, dim):
    return lax.broadcasted_iota(I32, shape, dim)


def grads(query, grad, key, value, lse_row, delta_row, allowed, scale):
    scores = dot(key, query, 1, 1) * scale
    probs = jnp.where(allowed, jnp.exp(scores - lse_row), 0.0)
    dprobs = dot(value, grad, 1, 1)
    dscores = (probs * (dprobs - delta_row)).astype(BF16)
    part_value = dot(probs.astype(BF16), grad, 1, 0)
    part_key = dot(dscores, query, 1, 0) * scale
    grad_query = dot(dscores, key, 0, 0) * scale
    return grad_query, part_key, part_value


def kernel(
    nh, nc, B, R, D, S, lane_rows,
    q_ref, k_ref, v_ref, g_ref, o_ref, lse_ref, sel_ref, docs_ref,
    gq_out, gk_out, gv_out,
    xq, xk, xv, xg, curq, curk, curv, curg, snd, far, gqs, gqr, curr, gqown, parts, own, run,
    go, dsend, dr, dl, auxs, auxr, selown, selall, meta, meta_s, bsel,
    xs, xr, fs, fr, gs, gr, ds, dsr, as_, ar, ss, sr, ls,
):
    h, c = lax.axis_index("head"), lax.axis_index("ctx")
    rows = R // nh
    scale = D ** (-0.5)
    shift = int(math.log2(B))
    lanes = 128

    selall[...] = jnp.full(selall.shape, -1, I32)
    own_row, own_lane = iota(selown.shape, 0), iota(selown.shape, 1)
    sel_now = jnp.zeros(selown.shape, I32)
    for b in range(B):
        for e in range(2):
            sel_now = jnp.where((own_row == b) & (own_lane == e), sel_ref[e, b], sel_now)
    selown[...] = sel_now
    curr[pl.ds(c, 1)] = jnp.zeros((1, R, D), BF16)

    barrier = pltpu.get_barrier_semaphore()

    def greet_head(n):
        pl.semaphore_signal(barrier, inc=1, device_id=(lax.rem(h + n, nh), c), device_id_type=MESH)

    def greet_ctx(n):
        pl.semaphore_signal(barrier, inc=1, device_id=(h, lax.rem(c + n, nc)), device_id_type=MESH)

    loop(1, nh, greet_head)
    loop(1, nc, greet_ctx)
    go_copies = [
        pltpu.make_async_copy(ref, go.at[n], ls.at[n]) for n, ref in enumerate((g_ref, o_ref))
    ]
    for copy in go_copies:
        copy.start()

    def find(owner):
        found = 0
        for b in range(B):
            found = found + jnp.where(sel_ref[0, b] // B == owner, b, 0)
        bsel[owner] = jnp.minimum(found, B - 1)

    loop(0, nc, find)
    pl.semaphore_wait(barrier, nh + nc - 2)

    def wait_bytes(ref, sem):
        pltpu.make_async_copy(ref, ref, sem).wait()

    sources, places = (q_ref, g_ref, k_ref, v_ref), (xq, xg, xk, xv)

    def columns(to, s):
        return pl.ds(pl.multiple_of(to * (S * D) + s * D, D), D)

    here = pl.ds(pl.multiple_of(h * rows, rows), rows)

    def head_copy(a, s, n):
        to = h ^ n
        return pltpu.make_async_remote_copy(
            src_ref=sources[a].at[:, :, columns(to, s)],
            dst_ref=places[a].at[s, :, here, :],
            send_sem=xs.at[a],
            recv_sem=xr.at[a, s],
            device_id=(to, c),
            device_id_type=MESH,
        )

    def head_local(a, s):
        return pltpu.make_async_copy(
            sources[a].at[:, :, columns(h, s)], places[a].at[s, :, here, :], xr.at[a, s]
        )

    def head_start(pair, s):
        for a in pair:
            loop(1, nh, lambda n: head_copy(a, s, n).start())
            head_local(a, s).start()

    def head_wait(pair, s):
        for a in pair:
            wait_bytes(places[a].at[s], xr.at[a, s])

    def up(n):
        return lax.rem(c + n, nc)

    def down(n):
        return lax.rem(c + nc - n, nc)

    def sel_copy(n):
        return pltpu.make_async_remote_copy(
            src_ref=selown, dst_ref=selall.at[c], send_sem=ss.at[0], recv_sem=sr.at[0],
            device_id=(h, down(n)), device_id_type=MESH,
        )

    loop(1, nc, lambda n: sel_copy(n).start())
    head_start((0,), 0)
    head_start((1,), 0)

    for copy in go_copies:
        copy.wait()
    pick = (iota((8, S * D), 1) // D == iota((8, S * D), 0)).astype(BF16)

    def delta_rows(to):
        cols = pl.ds(pl.multiple_of(to * (S * D), S * D), S * D)
        prod = go[0, :, :, cols].astype(F32) * go[1, :, :, cols].astype(F32)
        prod = prod.reshape(B * rows, S * D)
        high = prod.astype(BF16)
        low = (prod - high.astype(F32)).astype(BF16)
        dsend[to] = dot(pick, high, 1, 1) + dot(pick, low, 1, 1)

    loop(0, nh, delta_rows)

    def delta_copy(n):
        to = lax.rem(h + n, nh)
        return pltpu.make_async_remote_copy(
            src_ref=dsend.at[to], dst_ref=dr.at[h], send_sem=ds.at[0], recv_sem=dsr.at[0],
            device_id=(to, c), device_id_type=MESH,
        )

    loop(1, nh, lambda n: delta_copy(n).start())
    dr[pl.ds(h, 1)] = dsend[pl.ds(h, 1)]

    def far_copy(s, n, to):
        return pltpu.make_async_remote_copy(
            src_ref=snd.at[s, to], dst_ref=far.at[s, c],
            send_sem=fs.at[n], recv_sem=fr.at[s, n], device_id=(h, to), device_id_type=MESH,
        )

    def first_copy(a, n, to):
        return pltpu.make_async_remote_copy(
            src_ref=snd.at[0, to, a], dst_ref=far.at[0, c, a],
            send_sem=fs.at[n], recv_sem=fr.at[0, n], device_id=(h, to), device_id_type=MESH,
        )

    def gather(s):
        for a in range(2):
            head_wait((a,), s)

            @pl.when(s < S - 1)
            def _():
                head_start((a,), s + 1)

            @pl.when(s == S - 1)
            def _():
                head_start((a + 2,), 0)

        @pl.when(s == S - 1)
        def _():
            head_start((2, 3), 1)

        curq[...] = xq[s]
        curg[...] = xg[s]

        def one(n):
            to = down(n)
            b = bsel[to]
            snd[s, to, 0] = curq[b]
            snd[s, to, 1] = curg[b]
            far_copy(s, n, to).start()

        loop(1, c + 1, one)

    gather(0)
    wait_bytes(dr.at[pl.ds(0, nh - 1)], dsr.at[0])
    for b in range(B):
        dl[b] = jnp.concatenate(
            [dr[n][:, b * rows : (b + 1) * rows] for n in range(nh)], axis=1
        )

    def aux_copy(to):
        return pltpu.make_async_remote_copy(
            src_ref=auxs.at[to], dst_ref=auxr.at[c], send_sem=as_.at[0], recv_sem=ar.at[0],
            device_id=(h, to), device_id_type=MESH,
        )

    def aux_send(n):
        to = down(n)
        b = bsel[to]
        auxs[to, 0:S, :] = lse_ref[b]
        auxs[to, S : 2 * S, :] = dl[b][0:S]
        aux_copy(to).start()

    loop(1, nc, aux_send)

    loop(1, S, gather)

    wait_bytes(selall.at[pl.ds(0, nc - 1)], sr.at[0])
    picks = selall[...]
    hit = (picks >> shift) == c
    block_sum = lambda terms: jnp.sum(jnp.where(hit, terms, 0), axis=1)
    used = block_sum(jnp.ones_like(picks))
    local = block_sum(picks & (B - 1))
    which = block_sum(iota(picks.shape, 1))
    source, lane = iota((nc, lanes), 0), iota((nc, lanes), 1)
    order = jnp.where(used > 0, local, B)
    order = jnp.where(source > c, order, B + 1)

    def across(column):
        return jnp.sum(jnp.where(lane == source, column, 0), axis=0, keepdims=True)

    def total(terms):
        return jnp.sum(terms.astype(I32), axis=1, keepdims=True)

    inside = lane < nc
    full = [order[:, e : e + 1] * (4 * nc) + 2 * source[:, :1] + e for e in range(2)]
    full_rows = [across(column) for column in full]
    ranks = [
        sum(total((row < column) & inside) for row in full_rows) for column in full
    ]
    rank_rows = [across(column) for column in ranks]
    order_rows = [across(order[:, e : e + 1]) for e in range(2)]
    spot, spot_lane = iota((2 * nc, lanes), 0), iota((2 * nc, lanes), 1)
    at = [(row == spot) & (spot_lane < nc) for row in rank_rows]
    unit_at = sum(total(jnp.where(at[e], 2 * spot_lane + e, 0)) for e in range(2))
    block_at = sum(total(jnp.where(at[e], order_rows[e], 0)) for e in range(2))
    block, block_lane = iota((8, lanes), 0), iota((8, lanes), 1)
    last = sum(total((row <= block) & (block_lane < nc)) for row in order_rows) - 1
    has = sum(total((row == block) & (block_lane < nc)) for row in order_rows)

    def table(shape_lane, items):
        out = jnp.zeros(shape_lane.shape, I32)
        for n, item in enumerate(items):
            out = jnp.where(shape_lane == n, item, out)
        return out

    meta[0 : 2 * nc] = table(spot_lane, (unit_at, block_at))
    meta[2 * nc : 3 * nc] = table(
        lane, (local[:, 0:1], local[:, 1:2], used[:, 0:1], which[:, 0:1])
    )
    meta[3 * nc : 3 * nc + 8] = table(block_lane, (jnp.maximum(last, 0), has))
    to_scalar = pltpu.make_async_copy(meta, meta_s, ls.at[0])
    to_scalar.start()
    to_scalar.wait()

    wait_bytes(auxr.at[pl.ds(0, nc - 1)], ar.at[0])

    def doc_of(positions):
        end, doc = 0, jnp.zeros(positions.shape, I32)
        for n in range(docs_ref.shape[0]):
            end = end + docs_ref[n]
            doc = doc + (positions >= end).astype(I32)
        return doc

    row_lane, row_sub = iota((1, R), 1), iota((R, 1), 0)
    causal = row_sub <= row_lane

    def back_copy(s, n, to):
        return pltpu.make_async_remote_copy(
            src_ref=gqs.at[s, to], dst_ref=gqr.at[s, c], send_sem=gs.at[n],
            recv_sem=gr.at[(s + 1) // S, n], device_id=(h, to), device_id_type=MESH,
        )

    def out_cols(s):
        return pl.ds(pl.multiple_of(s * D, D), D)

    def finish_query(s):
        def one(n):
            curr[pl.ds(down(n), 1)] = gqr[s, pl.ds(down(n), 1)]

        loop(1, c + 1, one)

        def add(b):
            owner = (sel_ref[0, b] // B) & (nc - 1)
            total = gqown[s, b] + curr[owner].astype(F32)
            gq_out[b, :, out_cols(s)] = total.astype(BF16)

        loop(0, B, add)

    def heads(s):
        for a in (2, 3):
            head_wait((a,), s)

            @pl.when(s < S - 2)
            def _():
                head_start((a,), s + 2)

        curk[...] = xk[s]
        curv[...] = xv[s]

        def own_block(b):
            docs_lane = doc_of((c * B + b) * R + row_lane)
            docs_sub = doc_of((c * B + b) * R + row_sub)
            allowed = causal & (docs_lane == docs_sub)
            grad_query, part_key, part_value = grads(
                xq[s, b], xg[s, b], xk[s, b], xv[s, b],
                lse_ref[b, pl.ds(s, 1), :], dl[b, pl.ds(s, 1), :], allowed, scale,
            )
            gqown[s, b] = grad_query
            own[0, b] = part_key
            own[1, b] = part_value

        loop(0, B, own_block)

        def far_block(n):
            d = up(n)
            far_copy(s, n, up(n)).wait_recv()
            used_here = meta_s[2 * nc + d, 2] > 0
            docs_lane = doc_of((d * B + meta_s[2 * nc + d, 3]) * R + row_lane)
            keys, values, docs_sub = [], [], []
            for e in range(2):
                j = meta_s[2 * nc + d, e] & (B - 1)
                keys.append(curk[j])
                values.append(curv[j])
                docs_sub.append(
                    jnp.where(used_here, doc_of((c * B + j) * R + row_sub), -1)
                )
            allowed = jnp.concatenate(docs_sub, axis=0) == docs_lane
            grad_query, part_key, part_value = grads(
                far[s, d, 0], far[s, d, 1],
                jnp.concatenate(keys, axis=0), jnp.concatenate(values, axis=0),
                auxr[d, pl.ds(s, 1), :], auxr[d, pl.ds(S + s, 1), :], allowed, scale,
            )
            gqs[s, d] = grad_query.astype(BF16)
            back_copy(s, n, d).start()
            for e in range(2):
                parts[0, 2 * d + e] = part_key[e * R : (e + 1) * R].astype(BF16)
                parts[1, 2 * d + e] = part_value[e * R : (e + 1) * R].astype(BF16)

        loop(1, nc - c, far_block)

        for w in range(2):
            def add_hit(m, total_so_far):
                unit, j = meta_s[m, 0] & (2 * nc - 1), meta_s[m, 1]
                before = jnp.where(m == 0, -1, meta_s[jnp.maximum(m - 1, 0), 1])
                base = jnp.where(j == before, total_so_far, own[w, j & (B - 1)])
                total_now = base + parts[w, unit].astype(F32)
                run[m] = total_now.astype(BF16)
                return total_now

            lax.fori_loop(0, 2 * (nc - 1 - c), add_hit, jnp.zeros((R, D), F32))

            def settle(j):
                reached = meta_s[3 * nc + j, 1] > 0
                (gk_out, gv_out)[w][j, :, out_cols(s)] = jnp.where(
                    reached, run[meta_s[3 * nc + j, 0] & (2 * nc - 1)], own[w, j].astype(BF16)
                )

            loop(0, B, settle)

    loop(0, S, heads)
    loop(1, c + 1, lambda n: wait_bytes(gqr.at[0 : S - 1, down(n)], gr.at[0, n]))
    loop(0, S - 1, finish_query)
    loop(1, c + 1, lambda n: wait_bytes(gqr.at[S - 1, down(n)], gr.at[1, n]))
    finish_query(S - 1)

    wait_bytes(selall.at[pl.ds(0, nc - 1)], ss.at[0])
    wait_bytes(auxs.at[pl.ds(0, nc - 1)], as_.at[0])
    wait_bytes(dsend.at[pl.ds(0, nh - 1)], ds.at[0])
    for a in range(4):
        wait_bytes(places[a].at[:, :, pl.ds(0, R - rows), :], xs.at[a])
    loop(1, c + 1, lambda n: wait_bytes(snd.at[:, down(n)], fs.at[n]))
    loop(1, nc - c, lambda n: wait_bytes(gqs.at[:, up(n)], gs.at[n]))


def body(queries, keys, values, grad_out, attn_out, lse, selected, doc_lengths):
    B, rows, columns = queries.shape
    S = lse.shape[1]
    nh, nc = lax.axis_size("head"), lax.axis_size("ctx")
    D = columns // (S * nh)
    R = rows * nh
    any_, vmem, smem = (
        pl.BlockSpec(memory_space=space) for space in (pl.ANY, pltpu.VMEM, pltpu.SMEM)
    )
    shape = (B, R, S * D)
    out = pltpu.VMEM(shape, BF16)
    dma = pltpu.SemaphoreType.DMA
    block = (R, D)
    scratch = [
        pltpu.VMEM((S, B) + block, BF16),
        pltpu.VMEM((S, B) + block, BF16),
        pltpu.VMEM((S, B) + block, BF16),
        pltpu.VMEM((S, B) + block, BF16),
        pltpu.VMEM((B,) + block, BF16),
        pltpu.VMEM((B,) + block, BF16),
        pltpu.VMEM((B,) + block, BF16),
        pltpu.VMEM((B,) + block, BF16),
        pltpu.VMEM((S, nc, 2) + block, BF16),
        pltpu.VMEM((S, nc, 2) + block, BF16),
        pltpu.VMEM((S, nc) + block, BF16),
        pltpu.VMEM((S, nc) + block, BF16),
        pltpu.VMEM((nc,) + block, BF16),
        pltpu.VMEM((S, B) + block, F32),
        pltpu.VMEM((2, 2 * nc) + block, BF16),
        pltpu.VMEM((2, B) + block, F32),
        pltpu.VMEM((2 * nc,) + block, BF16),
        pltpu.VMEM((2, B, rows, columns), BF16),
        pltpu.VMEM((nh, 8, B * rows), F32),
        pltpu.VMEM((nh, 8, B * rows), F32),
        pltpu.VMEM((B, 8, R), F32),
        pltpu.VMEM((nc, 2 * S, R), F32),
        pltpu.VMEM((nc, 2 * S, R), F32),
        pltpu.VMEM((B, 128), I32),
        pltpu.VMEM((nc, B, 128), I32),
        pltpu.VMEM((3 * nc + 8, 128), I32),
        pltpu.SMEM((3 * nc + 8, 128), I32),
        pltpu.SMEM((nc,), I32),
        dma((4,)),
        dma((4, S)),
        dma((nc,)),
        dma((S, nc)),
        dma((nc,)),
        dma((2, nc)),
        dma((1,)),
        dma((1,)),
        dma((1,)),
        dma((1,)),
        dma((1,)),
        dma((1,)),
        dma((2,)),
    ]
    return pl.pallas_call(
        functools.partial(kernel, nh, nc, B, R, D, S, 128),
        out_shape=(out, out, out),
        in_specs=[any_, any_, any_, any_, any_, vmem, smem, smem],
        out_specs=(vmem, vmem, vmem),
        scratch_shapes=scratch,
        compiler_params=pltpu.CompilerParams(
            collective_id=0, has_side_effects=True, vmem_limit_bytes=54 * 2**20
        ),
        name="block_grads",
    )(queries, keys, values, grad_out, attn_out, lse, selected.T, doc_lengths)


def solution(mesh):
    rows = P("ctx", "head", None)
    in_specs = (rows, rows, rows, rows, rows, rows, P("ctx", None), P())
    out_specs = (P("ctx", None, "head"),) * 3
    return jax.shard_map(body, mesh=mesh, in_specs=in_specs, out_specs=out_specs, check_vma=False)
```

```python
import functools
import math

import jax
import jax.numpy as jnp
from jax import lax
from jax.experimental import pallas as pl
from jax.experimental.pallas import tpu as pltpu
from jax.sharding import PartitionSpec as P

MESH = pl.DeviceIdType.MESH
LOG2E = math.log2(math.e)
F32, BF16, I32 = jnp.float32, jnp.bfloat16, jnp.int32


def dot(left, right, left_dim, right_dim):
    return lax.dot_general(
        left, right, (((left_dim,), (right_dim,)), ((), ())), preferred_element_type=F32
    )


def loop(low, high, func):
    def step(index, carry):
        func(index)
        return carry

    lax.fori_loop(low, high, step, 0)


def iota(shape, dim):
    return lax.broadcasted_iota(I32, shape, dim)


def grads(query, grad, key, value, lse_row, delta_row, allowed, scale):
    scores = dot(key, query, 1, 1) * (scale * LOG2E)
    probs = jnp.where(allowed, jnp.exp2(scores - lse_row * LOG2E), 0.0)
    dprobs = dot(value, grad, 1, 1)
    dscores = (probs * (dprobs - delta_row)).astype(BF16)
    part_value = dot(probs.astype(BF16), grad, 1, 0)
    part_key = dot(dscores, query, 1, 0) * scale
    grad_query = dot(dscores, key, 0, 0) * scale
    return grad_query, part_key, part_value


def kernel(
    nh, nc, B, R, D, S, lane_rows,
    q_ref, k_ref, v_ref, g_ref, o_ref, lse_ref, sel_ref, docs_ref,
    gq_out, gk_out, gv_out,
    xq, xk, xv, xg, curq, curk, curv, curg, snd, far, gqs, gqr, curr, gqown, parts, own, run,
    go, dsend, dr, dl, auxs, auxr, selown, selall, meta, meta_s, bsel,
    xs, xr, fs, fr, gs, gr, ds, dsr, as_, ar, ss, sr, ls,
):
    h, c = lax.axis_index("head"), lax.axis_index("ctx")
    rows = R // nh
    scale = D ** (-0.5)
    shift = int(math.log2(B))
    lanes = 128

    selall[...] = jnp.full(selall.shape, -1, I32)
    curr[pl.ds(c, 1)] = jnp.zeros((1, R, D), BF16)

    barrier = pltpu.get_barrier_semaphore()

    def greet_head(n):
        pl.semaphore_signal(barrier, inc=1, device_id=(lax.rem(h + n, nh), c), device_id_type=MESH)

    def greet_ctx(n):
        pl.semaphore_signal(barrier, inc=1, device_id=(h, lax.rem(c + n, nc)), device_id_type=MESH)

    loop(1, nh, greet_head)
    loop(1, nc, greet_ctx)
    go_copies = [
        pltpu.make_async_copy(ref, go.at[n], ls.at[n]) for n, ref in enumerate((g_ref, o_ref))
    ]
    def find(owner):
        found = 0
        for b in range(B):
            found = found + jnp.where(sel_ref[0, b] // B == owner, b, 0)
        bsel[owner] = jnp.minimum(found, B - 1)

    loop(0, nc, find)
    own_row, own_lane = iota(selown.shape, 0), iota(selown.shape, 1)
    sel_now = jnp.zeros(selown.shape, I32)
    for b in range(B):
        for e in range(2):
            sel_now = jnp.where((own_row == b) & (own_lane == e), sel_ref[e, b], sel_now)
    selown[...] = sel_now
    pl.semaphore_wait(barrier, nh + nc - 2)

    def wait_bytes(ref, sem):
        pltpu.make_async_copy(ref, ref, sem).wait()

    sources, places = (q_ref, g_ref, k_ref, v_ref), (xq, xg, xk, xv)

    def columns(to, s):
        return pl.ds(pl.multiple_of(to * (S * D) + s * D, D), D)

    here = pl.ds(pl.multiple_of(h * rows, rows), rows)

    def head_copy(a, s, n):
        to = h ^ n
        return pltpu.make_async_remote_copy(
            src_ref=sources[a].at[:, :, columns(to, s)],
            dst_ref=places[a].at[s, :, here, :],
            send_sem=xs.at[a],
            recv_sem=xr.at[a, s],
            device_id=(to, c),
            device_id_type=MESH,
        )

    def head_local(a, s):
        return pltpu.make_async_copy(
            sources[a].at[:, :, columns(h, s)], places[a].at[s, :, here, :], xr.at[a, s]
        )

    def head_start(pair, s):
        for a in pair:
            loop(1, nh, lambda n: head_copy(a, s, n).start())
            head_local(a, s).start()

    def head_wait(pair, s):
        for a in pair:
            wait_bytes(places[a].at[s], xr.at[a, s])

    def up(n):
        return lax.rem(c + n, nc)

    def down(n):
        return lax.rem(c + nc - n, nc)

    def sel_copy(n):
        return pltpu.make_async_remote_copy(
            src_ref=selown, dst_ref=selall.at[c], send_sem=ss.at[0], recv_sem=sr.at[0],
            device_id=(h, down(n)), device_id_type=MESH,
        )

    head_start((0,), 0)
    head_start((1,), 0)
    for copy in go_copies:
        copy.start()
    loop(1, nc, lambda n: sel_copy(n).start())

    for copy in go_copies:
        copy.wait()
    pick = (iota((8, S * D), 1) // D == iota((8, S * D), 0)).astype(BF16)

    def delta_rows(to):
        cols = pl.ds(pl.multiple_of(to * (S * D), S * D), S * D)
        prod = go[0, :, :, cols].astype(F32) * go[1, :, :, cols].astype(F32)
        prod = prod.reshape(B * rows, S * D)
        high = prod.astype(BF16)
        low = (prod - high.astype(F32)).astype(BF16)
        dsend[to] = dot(pick, high, 1, 1) + dot(pick, low, 1, 1)

    loop(0, nh, delta_rows)

    def delta_copy(n):
        to = lax.rem(h + n, nh)
        return pltpu.make_async_remote_copy(
            src_ref=dsend.at[to], dst_ref=dr.at[h], send_sem=ds.at[0], recv_sem=dsr.at[0],
            device_id=(to, c), device_id_type=MESH,
        )

    loop(1, nh, lambda n: delta_copy(n).start())
    dr[pl.ds(h, 1)] = dsend[pl.ds(h, 1)]

    def far_copy(s, n, to):
        return pltpu.make_async_remote_copy(
            src_ref=snd.at[s, to], dst_ref=far.at[s, c],
            send_sem=fs.at[n], recv_sem=fr.at[s, n], device_id=(h, to), device_id_type=MESH,
        )

    def first_copy(a, n, to):
        return pltpu.make_async_remote_copy(
            src_ref=snd.at[0, to, a], dst_ref=far.at[0, c, a],
            send_sem=fs.at[n], recv_sem=fr.at[0, n], device_id=(h, to), device_id_type=MESH,
        )

    def gather(s):
        for a in range(2):
            head_wait((a,), s)

            @pl.when(s < S - 1)
            def _():
                head_start((a,), s + 1)

            @pl.when(s == S - 1)
            def _():
                head_start((a + 2,), 0)

        @pl.when(s == S - 1)
        def _():
            head_start((2, 3), 1)

        curq[...] = xq[s]
        curg[...] = xg[s]

        def one(n):
            to = down(n)
            b = bsel[to]
            snd[s, to, 0] = curq[b]
            snd[s, to, 1] = curg[b]

        loop(1, c + 1, one)
        loop(1, c + 1, lambda n: far_copy(s, n, down(n)).start())

    gather(0)
    wait_bytes(dr.at[pl.ds(0, nh - 1)], dsr.at[0])
    for b in range(B):
        dl[b] = jnp.concatenate(
            [dr[n][:, b * rows : (b + 1) * rows] for n in range(nh)], axis=1
        )

    def aux_copy(to):
        return pltpu.make_async_remote_copy(
            src_ref=auxs.at[to], dst_ref=auxr.at[c], send_sem=as_.at[0], recv_sem=ar.at[0],
            device_id=(h, to), device_id_type=MESH,
        )

    def aux_send(n):
        to = down(n)
        b = bsel[to]
        auxs[to, 0:S, :] = lse_ref[b]
        auxs[to, S : 2 * S, :] = dl[b][0:S]
        aux_copy(to).start()

    loop(1, nc, aux_send)

    loop(1, S, gather)

    wait_bytes(selall.at[pl.ds(0, nc - 1)], sr.at[0])
    picks = selall[...]
    hit = (picks >> shift) == c
    block_sum = lambda terms: jnp.sum(jnp.where(hit, terms, 0), axis=1)
    used = block_sum(jnp.ones_like(picks))
    local = block_sum(picks & (B - 1))
    which = block_sum(iota(picks.shape, 1))
    source, lane = iota((nc, lanes), 0), iota((nc, lanes), 1)
    order = jnp.where(used > 0, local, B)
    order = jnp.where(source > c, order, B + 1)

    def across(column):
        return jnp.sum(jnp.where(lane == source, column, 0), axis=0, keepdims=True)

    def total(terms):
        return jnp.sum(terms.astype(I32), axis=1, keepdims=True)

    inside = lane < nc
    full = [order[:, e : e + 1] * (4 * nc) + 2 * source[:, :1] + e for e in range(2)]
    full_rows = [across(column) for column in full]
    ranks = [
        sum(total((row < column) & inside) for row in full_rows) for column in full
    ]
    rank_rows = [across(column) for column in ranks]
    order_rows = [across(order[:, e : e + 1]) for e in range(2)]
    spot, spot_lane = iota((2 * nc, lanes), 0), iota((2 * nc, lanes), 1)
    at = [(row == spot) & (spot_lane < nc) for row in rank_rows]
    unit_at = sum(total(jnp.where(at[e], 2 * spot_lane + e, 0)) for e in range(2))
    block_at = sum(total(jnp.where(at[e], order_rows[e], 0)) for e in range(2))
    block, block_lane = iota((8, lanes), 0), iota((8, lanes), 1)
    last = sum(total((row <= block) & (block_lane < nc)) for row in order_rows) - 1
    has = sum(total((row == block) & (block_lane < nc)) for row in order_rows)

    def table(shape_lane, items):
        out = jnp.zeros(shape_lane.shape, I32)
        for n, item in enumerate(items):
            out = jnp.where(shape_lane == n, item, out)
        return out

    meta[0 : 2 * nc] = table(spot_lane, (unit_at, block_at))
    meta[2 * nc : 3 * nc] = table(
        lane, (local[:, 0:1], local[:, 1:2], used[:, 0:1], which[:, 0:1])
    )
    meta[3 * nc : 3 * nc + 8] = table(block_lane, (jnp.maximum(last, 0), has))
    to_scalar = pltpu.make_async_copy(meta, meta_s, ls.at[0])
    to_scalar.start()
    to_scalar.wait()

    wait_bytes(auxr.at[pl.ds(0, nc - 1)], ar.at[0])

    def doc_of(positions):
        end, doc = 0, jnp.zeros(positions.shape, I32)
        for n in range(docs_ref.shape[0]):
            end = end + docs_ref[n]
            doc = doc + (positions >= end).astype(I32)
        return doc

    row_lane, row_sub = iota((1, R), 1), iota((R, 1), 0)
    causal = row_sub <= row_lane

    def back_copy(s, n, to):
        return pltpu.make_async_remote_copy(
            src_ref=gqs.at[s, to], dst_ref=gqr.at[s, c], send_sem=gs.at[n],
            recv_sem=gr.at[jnp.maximum(s - 1, 0), n], device_id=(h, to), device_id_type=MESH,
        )

    def out_cols(s):
        return pl.ds(pl.multiple_of(s * D, D), D)

    def finish_query(s):
        def one(n):
            curr[pl.ds(down(n), 1)] = gqr[s, pl.ds(down(n), 1)]

        loop(1, c + 1, one)

        def add(b):
            owner = (sel_ref[0, b] // B) & (nc - 1)
            total = gqown[s, b] + curr[owner].astype(F32)
            gq_out[b, :, out_cols(s)] = total.astype(BF16)

        loop(0, B, add)

    def heads(s):
        for a in (2, 3):
            head_wait((a,), s)

            @pl.when(s < S - 2)
            def _():
                head_start((a,), s + 2)

        curk[...] = xk[s]
        curv[...] = xv[s]

        def own_block(b):
            docs_lane = doc_of((c * B + b) * R + row_lane)
            docs_sub = doc_of((c * B + b) * R + row_sub)
            allowed = causal & (docs_lane == docs_sub)
            grad_query, part_key, part_value = grads(
                xq[s, b], xg[s, b], xk[s, b], xv[s, b],
                lse_ref[b, pl.ds(s, 1), :], dl[b, pl.ds(s, 1), :], allowed, scale,
            )
            gqown[s, b] = grad_query
            own[0, b] = part_key
            own[1, b] = part_value

        loop(0, B, own_block)

        def far_block(n):
            d = up(n)
            far_copy(s, n, up(n)).wait_recv()
            used_here = meta_s[2 * nc + d, 2] > 0
            docs_lane = doc_of((d * B + meta_s[2 * nc + d, 3]) * R + row_lane)
            keys, values, docs_sub = [], [], []
            for e in range(2):
                j = meta_s[2 * nc + d, e] & (B - 1)
                keys.append(curk[j])
                values.append(curv[j])
                docs_sub.append(
                    jnp.where(used_here, doc_of((c * B + j) * R + row_sub), -1)
                )
            allowed = jnp.concatenate(docs_sub, axis=0) == docs_lane
            grad_query, part_key, part_value = grads(
                far[s, d, 0], far[s, d, 1],
                jnp.concatenate(keys, axis=0), jnp.concatenate(values, axis=0),
                auxr[d, pl.ds(s, 1), :], auxr[d, pl.ds(S + s, 1), :], allowed, scale,
            )
            gqs[s, d] = grad_query.astype(BF16)
            back_copy(s, n, d).start()
            for e in range(2):
                parts[0, 2 * d + e] = part_key[e * R : (e + 1) * R].astype(BF16)
                parts[1, 2 * d + e] = part_value[e * R : (e + 1) * R].astype(BF16)

        @pl.when(s == S - 1)
        def _():
            loop(1, c + 1, lambda n: wait_bytes(gqr.at[0 : S - 2, down(n)], gr.at[0, n]))
            loop(0, S - 2, finish_query)

        loop(1, nc - c, far_block)

        for w in range(2):
            def add_two(m, total_so_far):
                return add_hit(2 * m + 1, add_hit(2 * m, total_so_far))

            def add_hit(m, total_so_far):
                unit, j = meta_s[m, 0] & (2 * nc - 1), meta_s[m, 1]
                before = jnp.where(m == 0, -1, meta_s[jnp.maximum(m - 1, 0), 1])
                base = jnp.where(j == before, total_so_far, own[w, j & (B - 1)])
                total_now = base + parts[w, unit].astype(F32)
                run[m] = total_now.astype(BF16)
                return total_now

            lax.fori_loop(0, nc - 1 - c, add_two, jnp.zeros((R, D), F32))

            def settle(j):
                reached = meta_s[3 * nc + j, 1] > 0
                (gk_out, gv_out)[w][j, :, out_cols(s)] = jnp.where(
                    reached, run[meta_s[3 * nc + j, 0] & (2 * nc - 1)], own[w, j].astype(BF16)
                )

            loop(0, B, settle)

    loop(0, S, heads)
    for t in (S - 2, S - 1):
        loop(1, c + 1, lambda n: wait_bytes(gqr.at[t, down(n)], gr.at[t - 1, n]))
        finish_query(t)

    wait_bytes(selall.at[pl.ds(0, nc - 1)], ss.at[0])
    wait_bytes(auxs.at[pl.ds(0, nc - 1)], as_.at[0])
    wait_bytes(dsend.at[pl.ds(0, nh - 1)], ds.at[0])
    for a in range(4):
        wait_bytes(places[a].at[:, :, pl.ds(0, R - rows), :], xs.at[a])
    loop(1, c + 1, lambda n: wait_bytes(snd.at[:, down(n)], fs.at[n]))
    loop(1, nc - c, lambda n: wait_bytes(gqs.at[:, up(n)], gs.at[n]))


def body(queries, keys, values, grad_out, attn_out, lse, selected, doc_lengths):
    B, rows, columns = queries.shape
    S = lse.shape[1]
    nh, nc = lax.axis_size("head"), lax.axis_size("ctx")
    D = columns // (S * nh)
    R = rows * nh
    any_, vmem, smem = (
        pl.BlockSpec(memory_space=space) for space in (pl.ANY, pltpu.VMEM, pltpu.SMEM)
    )
    shape = (B, R, S * D)
    out = pltpu.VMEM(shape, BF16)
    dma = pltpu.SemaphoreType.DMA
    block = (R, D)
    scratch = [
        pltpu.VMEM((S, B) + block, BF16),
        pltpu.VMEM((S, B) + block, BF16),
        pltpu.VMEM((S, B) + block, BF16),
        pltpu.VMEM((S, B) + block, BF16),
        pltpu.VMEM((B,) + block, BF16),
        pltpu.VMEM((B,) + block, BF16),
        pltpu.VMEM((B,) + block, BF16),
        pltpu.VMEM((B,) + block, BF16),
        pltpu.VMEM((S, nc, 2) + block, BF16),
        pltpu.VMEM((S, nc, 2) + block, BF16),
        pltpu.VMEM((S, nc) + block, BF16),
        pltpu.VMEM((S, nc) + block, BF16),
        pltpu.VMEM((nc,) + block, BF16),
        pltpu.VMEM((S, B) + block, F32),
        pltpu.VMEM((2, 2 * nc) + block, BF16),
        pltpu.VMEM((2, B) + block, F32),
        pltpu.VMEM((2 * nc,) + block, BF16),
        pltpu.VMEM((2, B, rows, columns), BF16),
        pltpu.VMEM((nh, 8, B * rows), F32),
        pltpu.VMEM((nh, 8, B * rows), F32),
        pltpu.VMEM((B, 8, R), F32),
        pltpu.VMEM((nc, 2 * S, R), F32),
        pltpu.VMEM((nc, 2 * S, R), F32),
        pltpu.VMEM((B, 128), I32),
        pltpu.VMEM((nc, B, 128), I32),
        pltpu.VMEM((3 * nc + 8, 128), I32),
        pltpu.SMEM((3 * nc + 8, 128), I32),
        pltpu.SMEM((nc,), I32),
        dma((4,)),
        dma((4, S)),
        dma((nc,)),
        dma((S, nc)),
        dma((nc,)),
        dma((3, nc)),
        dma((1,)),
        dma((1,)),
        dma((1,)),
        dma((1,)),
        dma((1,)),
        dma((1,)),
        dma((2,)),
    ]
    return pl.pallas_call(
        functools.partial(kernel, nh, nc, B, R, D, S, 128),
        out_shape=(out, out, out),
        in_specs=[any_, any_, any_, any_, any_, vmem, smem, smem],
        out_specs=(vmem, vmem, vmem),
        scratch_shapes=scratch,
        compiler_params=pltpu.CompilerParams(
            collective_id=0, has_side_effects=True, vmem_limit_bytes=54 * 2**20
        ),
        name="block_grads",
    )(queries, keys, values, grad_out, attn_out, lse, selected.T, doc_lengths)


def solution(mesh):
    rows = P("ctx", "head", None)
    in_specs = (rows, rows, rows, rows, rows, rows, P("ctx", None), P())
    out_specs = (P("ctx", None, "head"),) * 3
    return jax.shard_map(body, mesh=mesh, in_specs=in_specs, out_specs=out_specs, check_vma=False)
```
